32 devices in a mesh: dp: 8 (over y, x, core), mp: 4 (over z).
Axes of the slice: x: 2, y: 2, z: 4, core: 2. Of those that a mesh axis runs over, the one named last changes fastest.
Arguments:
- tokens: bfloat16 [12288, 768], P('dp'), may hold values from -6 to 6
- segment_ids: int32 [24, 512], P('dp'), may hold values from 0 to 3, never falling along the last dimension, each value on 1 to 256 neighbouring positions
- lengths: int32 [24], P('dp'), may hold values from 256 to 512, as said below
- cotangent: float32 [12288], P('dp'), may hold values from -6 to 6
- w_qkv: bfloat16 [768, 3, 768], P(None, None, 'mp'), may hold values from -0.21875 to 0.21875
- b_qv: bfloat16 [2, 768], P(None, 'mp'), may hold values from -3 to 3
- w_out: bfloat16 [768, 768], P('mp'), may hold values from -1.25 to 1.25
- b_out: bfloat16 [768], replicated, may hold values from -3 to 3
- gain_one: bfloat16 [768], replicated, may hold values from 0.5 to 1.5
- shift_one: bfloat16 [768], replicated, may hold values from -1.75 to 1.75
- w_up: bfloat16 [768, 3072], P(None, 'mp'), may hold values from -0.21875 to 0.21875
- b_up: bfloat16 [3072], P('mp'), may hold values from -3 to 3
- w_down: bfloat16 [3072, 768], P('mp'), may hold values from -0.15625 to 0.15625
- b_down: bfloat16 [768], replicated, may hold values from -3 to 3
- gain_two: bfloat16 [768], replicated, may hold values from 0.5 to 1.5
- w_head: bfloat16 [768], replicated, may hold values from -0.21875 to 0.21875
- b_head: bfloat16 [1], replicated, may hold values from -6 to 6
Outputs:
- token_weight: float32 [12288], P('dp')
- input_grad: float32 [12288, 768], P('dp')
- grad_qkv: float32 [768, 3, 768], P(None, None, 'mp')
- grad_qv_bias: float32 [2, 768], P(None, 'mp')
- grad_out: float32 [768, 768], P('mp')
- grad_out_bias: float32 [768], replicated
- grad_gain_one: float32 [768], replicated
- grad_shift_one: float32 [768], replicated
- grad_up: float32 [768, 3072], P(None, 'mp')
- grad_up_bias: float32 [3072], P('mp')
- grad_down: float32 [3072, 768], P('mp')
- grad_down_bias: float32 [768], replicated
- grad_gain_two: float32 [768], replicated
- grad_head: float32 [768], replicated
- grad_head_bias: float32 [1], replicated
The draws below stay inside these ranges and needn't reach their ends.
Inputs may be any that keep to these rules, and one draw needn't show every extreme that they name: `lengths`: one packed row of each draw is full and one holds 256 tokens before its padding. `segment_ids`: non-decreasing along each packed row.
All inputs are finite; a program needn't handle non-finite values.
Results may differ from the reference program's by a relative error of at most 0.015.
Values sent between devices are 32-bit elements; how exact they have to be, the bound alone decides.
No kernel may reach another device: no remote copies, remote signals or barrier semaphores. Data moves between devices by JAX's collectives and lax.ppermute only.
A program may use at most 128 MiB of HBM per device.

```python
import math
import jax
import jax.numpy as jnp
import numpy as np
from jax import lax

D = 768
HEADS = 12
HEAD = 64
FF = 3072
SEQ = 512
ROWS = 24
TOKENS = 12288


def draw_lengths(key, part):
    key = jax.random.fold_in(key, 7)
    first_key, second_key = jax.random.split(key, 2)
    cut_back = jax.random.randint(first_key, (ROWS,), 0, SEQ // 2 + 1)
    order = jax.random.permutation(second_key, ROWS)
    cut_back = jnp.where(order == 0, 0, cut_back)
    cut_back = jnp.where(order == 1, SEQ // 2, cut_back)
    return (SEQ - cut_back).astype(jnp.int32)


def levels(rng, extent, cuts, smallest, high):
    def one(axis_at, blocks):
        steps = jax.random.uniform(jax.random.fold_in(jax.random.fold_in(rng, 6), axis_at), (blocks,), jnp.float32, smallest / len(cuts), high / len(cuts))
        return jnp.repeat(jnp.exp(steps), extent[axis_at] // blocks).reshape((-1,) + (1,) * (len(extent) - axis_at - 1))

    level = one(*cuts[0])
    for cut in cuts[1:]:
        level = level * one(*cut)
    return level


def length_profile(amount, total, bound, lean):
    loads = [(1 << 20) // math.isqrt(standing ** lean) + 1 for standing in range(2, amount + 1)]
    surplus, holding = total - bound - (amount - 1), [1] * (amount - 1)
    while surplus > 0:
        free = [i for i in range(amount - 1) if holding[i] < bound]
        mass, budget = sum([loads[i] for i in free]), surplus
        for i in free:
            more = min(bound - holding[i], max(1, budget * loads[i] // mass), surplus)
            holding[i] = holding[i] + more
            surplus = surplus - more
    return np.array([bound] + holding)


def uneven_parts(rng, count, total, limit, skew):
    if count == 2:
        one = jax.random.randint(rng, (), max(1, total - limit), min(limit, total - 1) + 1)
        return jnp.stack([one, total - one])
    sizes = jnp.asarray(length_profile(count, total, limit, skew), jnp.int32)
    couples = (count - 1) // 2
    source_of, receiver = sizes[1:1 + 2 * couples:2], sizes[2:2 + 2 * couples:2]
    margin = jnp.minimum(source_of - 1, limit - receiver)
    shifted = jax.random.randint(jax.random.fold_in(rng, 1), (couples,), 0, 1 << 20) % (margin + 1)
    sizes = sizes.at[1:1 + 2 * couples:2].set(source_of - shifted).at[2:2 + 2 * couples:2].set(receiver + shifted)
    return sizes[jax.random.permutation(jax.random.fold_in(rng, 2), count)]


def scatter_about(rng, shape, width, limit, shards=(), kind=jnp.bfloat16):
    values = width * jax.random.normal(rng, shape, jnp.float32)
    if shards:
        values = values * levels(rng, shape, shards, -0.22, 0.18)
    return jnp.clip(values, -limit, limit).astype(kind)


def setup_inputs(seed: int = 0) -> dict:
    arg_keys = jax.random.split(jax.random.key(seed), 18)
    return {
        "tokens": scatter_about(arg_keys[0], (TOKENS, D), 1.0, 6.0, ((0, 8),)),
        "segment_ids": jax.vmap(lambda own: jnp.searchsorted(jnp.cumsum(uneven_parts(own, 4, SEQ, SEQ // 2, 0)), jnp.arange(SEQ), side="right"))(jax.random.split(arg_keys[1], ROWS)).reshape((ROWS, SEQ)).astype(jnp.int32),
        "lengths": draw_lengths(jax.random.fold_in(arg_keys[17], 71), 0),
        "cotangent": scatter_about(arg_keys[3], (TOKENS,), 1.0, 6.0, ((0, 8),), jnp.float32),
        "w_qkv": scatter_about(arg_keys[4], (D, 3, D), D ** -0.5, 0.21875, ((2, 4),)),
        "b_qv": scatter_about(arg_keys[5], (2, D), 0.5, 3.0, ((1, 4),)),
        "w_out": scatter_about(arg_keys[6], (D, D), (D * 16 // SEQ) ** -0.5, 1.25, ((0, 4),)),
        "b_out": scatter_about(arg_keys[7], (D,), 0.5, 3.0),
        "gain_one": jnp.clip(1.0 + 0.1 * jax.random.normal(arg_keys[8], (D,), jnp.float32), 0.5, 1.5).astype(jnp.bfloat16),
        "shift_one": scatter_about(arg_keys[9], (D,), 0.3, 1.75),
        "w_up": scatter_about(arg_keys[10], (D, FF), D ** -0.5, 0.21875, ((1, 4),)),
        "b_up": scatter_about(arg_keys[11], (FF,), 0.5, 3.0, ((0, 4),)),
        "w_down": scatter_about(arg_keys[12], (FF, D), (FF // 2) ** -0.5, 0.15625, ((0, 4),)),
        "b_down": scatter_about(arg_keys[13], (D,), 0.5, 3.0),
        "gain_two": jnp.clip(1.0 + 0.1 * jax.random.normal(arg_keys[14], (D,), jnp.float32), 0.5, 1.5).astype(jnp.bfloat16),
        "w_head": scatter_about(arg_keys[15], (D,), D ** -0.5, 0.21875),
        "b_head": scatter_about(arg_keys[16], (1,), 1.0, 6.0),
    }


@jax.custom_vjp
def low(v):
    return lax.optimization_barrier(v.astype(jnp.bfloat16)).astype(jnp.float32)

@jax.custom_vjp
def low_back(v):
    return v

def low_keep(v):
    return (low(v), None)

def low_pass(kept, grad):
    return (grad,)

def back_keep(v):
    return (v, None)

def back_low(kept, grad):
    return (low(grad),)
low.defvjp(low_keep, low_pass)
low_back.defvjp(back_keep, back_low)
norm_eps = 1e-12
highest = lax.Precision.HIGHEST

def layer_norm(residual, gain_vec, shift_vec):
    row_mean = lax.optimization_barrier(jnp.mean(residual, axis=-1, keepdims=True))
    centered = residual - row_mean
    variance = lax.optimization_barrier(jnp.mean(centered * centered, axis=-1, keepdims=True))
    return centered * lax.rsqrt(variance + norm_eps) * gain_vec + shift_vec

def gelu_exact(values_in):
    return 0.5 * values_in * (1.0 + lax.erf(values_in * 0.7071067811865476))

def attend_row(packed):
    query_rows, key_rows, value_rows, segments, length = packed
    positions = jnp.arange(SEQ)
    allowed = (segments[:, None] == segments[None, :]) & ((positions[None, :] < length) | (positions[:, None] == positions[None, :]))
    scores = low_back(jnp.einsum('qhe,khe->hqk', query_rows, key_rows, precision=highest) * HEAD ** (-0.5))
    scores = jnp.where(allowed[None], scores, -1e+30)
    row_max = lax.optimization_barrier(jnp.max(scores, axis=-1, keepdims=True))
    exponent = jnp.exp(scores - row_max)
    attn_weights = exponent / lax.optimization_barrier(jnp.sum(exponent, axis=-1, keepdims=True))
    return jnp.einsum('hqk,khe->qhe', low(attn_weights), value_rows, precision=highest)

def forward(tokens, w_qkv, b_qv, w_out, b_out, gain_one, shift_one, w_up, b_up, w_down, b_down, gain_two, w_head, b_head, segment_ids, lengths):
    projected = jnp.einsum('td,dcn->tcn', low(tokens), w_qkv, precision=highest)
    query_all = low(low_back(projected[:, 0] + b_qv[0]))
    key_all = low(low_back(projected[:, 1]))
    value_all = low(low_back(projected[:, 2] + b_qv[1]))
    row_shape = (ROWS, SEQ, HEADS, HEAD)
    context = lax.map(jax.checkpoint(attend_row), (query_all.reshape(row_shape), key_all.reshape(row_shape), value_all.reshape(row_shape), segment_ids, lengths))
    context = context.reshape(TOKENS, D)
    branch = low_back(jnp.dot(low(context), w_out, precision=highest))
    norm_one = layer_norm(tokens + branch + b_out, gain_one, shift_one)
    hidden_pre = low_back(jnp.dot(low(norm_one), w_up, precision=highest)) + b_up
    down_out = low_back(jnp.dot(low(gelu_exact(hidden_pre)), w_down, precision=highest))
    norm_two = layer_norm(norm_one + down_out + b_down, gain_two, 0.0)
    logits = jnp.dot(norm_two, w_head, precision=highest) + b_head[0]
    positions = jnp.arange(SEQ)
    valid_mask = (positions[None, :] < lengths[:, None]).reshape(TOKENS).astype(jnp.float32)
    return jax.nn.softplus(logits) * valid_mask

def reference(tokens, segment_ids, lengths, cotangent, w_qkv, b_qv, w_out, b_out, gain_one, shift_one, w_up, b_up, w_down, b_down, gain_two, w_head, b_head):
    floats = [array_in.astype(jnp.float32) for array_in in (tokens, w_qkv, b_qv, w_out, b_out, gain_one, shift_one, w_up, b_up, w_down, b_down, gain_two, w_head, b_head)]

    def wrapped(*arrays):
        return forward(*arrays, segment_ids, lengths)
    token_weight, pullback = jax.vjp(wrapped, *floats)
    gradients = pullback(cotangent.astype(jnp.float32))
    return (token_weight, gradients[0], gradients[1], gradients[2], gradients[3], gradients[4], gradients[5], gradients[6], gradients[7], gradients[8], gradients[9], gradients[10], gradients[11], gradients[12], gradients[13])
```

```python
import functools

import jax
import jax.numpy as jnp
from jax import lax
from jax.experimental import pallas as pl
from jax.experimental.pallas import tpu as pltpu
from jax.sharding import PartitionSpec as P

HEAD = 64
CORE = 1
norm_eps = 1e-12
highest = lax.Precision.HIGHEST
f32 = jnp.float32
bf16 = jnp.bfloat16


def dot(left, right, left_dim, right_dim):
    return lax.dot_general(
        left, right, (((left_dim,), (right_dim,)), ((), ())), preferred_element_type=f32
    )


def layer_norm(residual, gain_vec):
    row_mean = jnp.mean(residual, axis=-1, keepdims=True)
    centered = residual - row_mean
    inv_std = lax.rsqrt(jnp.mean(centered * centered, axis=-1, keepdims=True) + norm_eps)
    normed = centered * inv_std
    return (normed * gain_vec, normed, inv_std)


def norm_back(grad_rows, normed, inv_std, gain_vec):
    grad_normed = grad_rows * gain_vec
    grad_res = (
        grad_normed
        - jnp.mean(grad_normed, axis=-1, keepdims=True)
        - normed * jnp.mean(grad_normed * normed, axis=-1, keepdims=True)
    ) * inv_std
    return (grad_res, jnp.sum(grad_rows * normed, axis=0), jnp.sum(grad_rows, axis=0))


def gelu_exact(values_in):
    return 0.5 * values_in * (1.0 + lax.erf(values_in * 0.7071067811865476))


def gelu_slope(values_in):
    return (
        0.5 * (1.0 + lax.erf(values_in * 0.7071067811865476))
        + values_in * jnp.exp(-0.5 * values_in * values_in) * 0.3989422804014327
    )


def attend_kernel(qkv_ref, mask_ref, context_ref, probs_ref):
    query, key, value = qkv_ref[0, 0], qkv_ref[1, 0], qkv_ref[2, 0]
    scores = dot(key, query, 0, 0) + mask_ref[...]
    exponent = jnp.exp(scores - jnp.max(scores, axis=0, keepdims=True))
    total = jnp.sum(exponent, axis=0, keepdims=True)
    probs = (exponent / total).astype(bf16)
    probs_ref[0] = probs
    context_ref[0] = dot(value, probs, 1, 0).astype(bf16)


def attend(qkv, mask):
    heads, head, seq = qkv.shape[1:]
    return pl.pallas_call(
        attend_kernel,
        grid=(heads,),
        in_specs=[
            pl.BlockSpec((3, 1, head, seq), lambda h: (0, h, 0, 0)),
            pl.BlockSpec((seq, seq), lambda h: (0, 0)),
        ],
        out_specs=[
            pl.BlockSpec((1, head, seq), lambda h: (h, 0, 0)),
            pl.BlockSpec((1, seq, seq), lambda h: (h, 0, 0)),
        ],
        out_shape=[
            jax.ShapeDtypeStruct((heads, head, seq), bf16),
            jax.ShapeDtypeStruct((heads, seq, seq), bf16),
        ],
        compiler_params=pltpu.CompilerParams(vmem_limit_bytes=24 << 20),
        cost_estimate=pl.CostEstimate(
            flops=16 * heads * seq * seq * head,
            bytes_accessed=4 * heads * seq * seq,
            transcendentals=heads * seq * seq,
        ),
        name="attend",
    )(qkv, mask)


def attend_back_kernel(qkv_ref, probs_ref, context_ref, grad_ref, out_ref):
    query, key, value = qkv_ref[0, 0], qkv_ref[1, 0], qkv_ref[2, 0]
    probs = probs_ref[0]
    grad = grad_ref[0]
    shared = jnp.sum(grad.astype(f32) * context_ref[0].astype(f32), axis=0, keepdims=True)
    d_probs = dot(value, grad, 0, 0)
    d_scores = (probs.astype(f32) * (d_probs - shared)).astype(bf16)
    out_ref[0, 0] = (dot(key, d_scores, 1, 0) * HEAD**-0.5).astype(bf16)
    out_ref[1, 0] = dot(query, d_scores, 1, 1).astype(bf16)
    out_ref[2, 0] = dot(grad, probs, 1, 1).astype(bf16)


def attend_back(qkv, probs, context, grad):
    heads, head, seq = qkv.shape[1:]
    return pl.pallas_call(
        attend_back_kernel,
        grid=(heads,),
        in_specs=[
            pl.BlockSpec((3, 1, head, seq), lambda h: (0, h, 0, 0)),
            pl.BlockSpec((1, seq, seq), lambda h: (h, 0, 0)),
            pl.BlockSpec((1, head, seq), lambda h: (h, 0, 0)),
            pl.BlockSpec((1, head, seq), lambda h: (h, 0, 0)),
        ],
        out_specs=pl.BlockSpec((3, 1, head, seq), lambda h: (0, h, 0, 0)),
        out_shape=jax.ShapeDtypeStruct(qkv.shape, bf16),
        compiler_params=pltpu.CompilerParams(vmem_limit_bytes=24 << 20),
        cost_estimate=pl.CostEstimate(
            flops=32 * heads * seq * seq * head,
            bytes_accessed=2 * heads * seq * seq,
            transcendentals=0,
        ),
        name="attend_back",
    )(qkv, probs, context, grad)


def ordered_kernel(order, own_ref, got_ref, out_ref):
    rows = [ref[at, 0] for ref in (own_ref, got_ref) for at in order]
    out_ref[0] = jnp.concatenate(rows).astype(bf16)


def ordered(held):
    own, got, masks = held
    order = sorted(range(len(masks)), key=lambda at: masks[at])
    if own.shape[2] % 8:
        own, got = (jnp.concatenate([a[at] for at in order], axis=1)[None] for a in (own, got))
        order = [0]
    chips, group, strip, width = own.shape
    cuts = 2 if group == 1 else 1
    block = pl.BlockSpec((chips, 1, strip, width // cuts), lambda g, w: (0, g, 0, w))
    return pl.pallas_call(
        functools.partial(ordered_kernel, order),
        grid=(group, cuts),
        in_specs=[block, block],
        out_specs=pl.BlockSpec((1, 2 * chips * strip, width // cuts), lambda g, w: (g, 0, w)),
        out_shape=jax.ShapeDtypeStruct((group, 2 * chips * strip, width), bf16),
        compiler_params=pltpu.CompilerParams(vmem_limit_bytes=24 << 20),
        cost_estimate=pl.CostEstimate(flops=0, bytes_accessed=10 * own.size, transcendentals=0),
        name="ordered",
    )(own, got)


def natural_kernel(masks, me_ref, own_ref, got_ref, out_ref):
    strip = own_ref.shape[2]
    for core, ref in enumerate((own_ref, got_ref)):
        for at, mask in enumerate(masks):
            start = pl.multiple_of((me_ref[0] ^ (mask | core)) * strip, 8)
            out_ref[0, pl.ds(start, strip)] = ref[at, 0]


def natural(held, me):
    own, got, masks = held
    chips, group, strip, width = own.shape
    if strip % 8:
        stacked = jnp.concatenate([own, got])
        spots = [masks.index(m & ~CORE) + chips * (m & CORE) for m in range(2 * chips)]
        stacked = jnp.stack([stacked[at] for at in spots])
        return jnp.concatenate(
            [lax.dynamic_index_in_dim(stacked, me ^ j, 0, keepdims=False) for j in range(2 * chips)],
            axis=1,
        )
    cuts = 2 if group == 1 else 1
    block = pl.BlockSpec((chips, 1, strip, width // cuts), lambda g, w: (0, g, 0, w))
    return pl.pallas_call(
        functools.partial(natural_kernel, masks),
        grid=(group, cuts),
        in_specs=[pl.BlockSpec(memory_space=pltpu.SMEM), block, block],
        out_specs=pl.BlockSpec((1, 2 * chips * strip, width // cuts), lambda g, w: (g, 0, w)),
        out_shape=jax.ShapeDtypeStruct((group, 2 * chips * strip, width), f32),
        compiler_params=pltpu.CompilerParams(vmem_limit_bytes=24 << 20),
        cost_estimate=pl.CostEstimate(flops=0, bytes_accessed=16 * own.size, transcendentals=0),
        name="natural",
    )(me.astype(jnp.int32)[None], own, got)


def hold(array):
    return lax.optimization_barrier(array)


class Links:
    def __init__(self, dp_size, mp_size):
        self.dp_size, self.mp_size = dp_size, mp_size
        chip_bits = [1 << b for b in range(1, dp_size.bit_length() - 1)]
        self.orders = (chip_bits, chip_bits[::-1])
        self.chip_masks = list(range(0, dp_size, 2))

    def swap(self, array, bit):
        return hold(lax.ppermute(hold(array), "dp", [(i, i ^ bit) for i in range(self.dp_size)]))

    def ring(self, array):
        size = self.mp_size
        return hold(lax.ppermute(hold(array), "mp", [(i, (i + 1) % size) for i in range(size)]))

    def gather(self, pieces):
        stacks = [piece[None] for piece in pieces]
        masks = [[0], [0]]
        for step in range(len(self.orders[0])):
            got = [self.swap(stack, self.orders[side][step]) for side, stack in enumerate(stacks)]
            for side in range(2):
                bit = self.orders[side][step]
                stacks[side] = jnp.concatenate([stacks[side], got[side]])
                masks[side] = masks[side] + [m ^ bit for m in masks[side]]
        return [(stack, self.swap(stack, CORE), order) for stack, order in zip(stacks, masks)]

    def scatter(self, parts, side):
        for bit in reversed(self.orders[side]):
            kept = [m for m in parts if not m & bit]
            got = self.swap(jnp.stack([parts[m | bit] for m in kept]), bit)
            parts = {m: parts[m] + got[at] for at, m in enumerate(kept)}
        return parts[0]


def body(
    tokens,
    segment_ids,
    lengths,
    cotangent,
    w_qkv,
    b_qv,
    w_out,
    b_out,
    gain_one,
    shift_one,
    w_up,
    b_up,
    w_down,
    b_down,
    gain_two,
    w_head,
    b_head,
    *,
    dp_size,
    mp_size,
):
    links = Links(dp_size, mp_size)
    row_count, seq = segment_ids.shape
    width = tokens.shape[1]
    local_width = w_qkv.shape[2]
    heads = local_width // HEAD
    hidden = w_up.shape[1]
    groups = 4 * heads
    half_groups = groups // 2
    strip = HEAD // dp_size
    span = hidden // dp_size
    me = lax.axis_index("dp")
    z = lax.axis_index("mp")
    masks = links.chip_masks + [m | CORE for m in links.chip_masks]
    half = dp_size // 2
    later = list(range(1, mp_size)) + [0]

    owners = [i for i in range(mp_size) if i != mp_size // 2][:row_count]
    row_of = [owners.index(i) if i in owners else 0 for i in range(mp_size)]
    row = jnp.asarray(row_of, jnp.int32)[z]
    active = jnp.asarray([float(i in owners) for i in range(mp_size)], f32)[z]

    attn_own = jnp.concatenate(
        [jnp.transpose(w_qkv, (1, 2, 0)).reshape(3 * heads, HEAD, width), w_out.reshape(heads, HEAD, width)]
    ).reshape(groups, dp_size, strip, width)
    up_own = w_up.T.reshape(dp_size, span, width)
    down_own = w_down.reshape(dp_size, span, width)

    def slice_of(array, at, axis):
        return lax.dynamic_index_in_dim(array, at, axis, keepdims=False)

    attn_mine = slice_of(attn_own, me, 1).astype(f32)
    ffn_mine = tuple(slice_of(own, me, 0).astype(f32)[None] for own in (up_own, down_own))
    pieces = {"attn": (attn_mine[:half_groups], attn_mine[half_groups:]), "ffn": ffn_mine}

    def own_order(array, axis):
        return jnp.concatenate(
            [lax.dynamic_slice_in_dim(array, me ^ m, 1, axis) for m in masks], axis=axis
        )

    attn_w = [own_order(attn_own, 1).reshape(groups, HEAD, width)]
    ffn_w = [
        [
            own_order(up_own, 0).reshape(hidden, width),
            own_order(down_own, 0).reshape(hidden, width),
        ]
    ]
    going = pieces["attn"]
    for k in range(1, mp_size):
        going = tuple(links.ring(piece) for piece in going)
        attn_w.append(jnp.concatenate([ordered(held) for held in links.gather(going)]))
    going = pieces["ffn"]
    for k in range(1, mp_size):
        going = tuple(links.ring(piece) for piece in going)
        ffn_w.append([ordered(held).reshape(hidden, width) for held in links.gather(going)])

    small = jnp.concatenate([b_qv.astype(f32).reshape(-1), b_up.astype(f32)])
    small = lax.all_gather(small, "mp")
    slice_pick = (
        jnp.asarray(masks, jnp.int32)[:, None] ^ me
    ) == jnp.arange(dp_size, dtype=jnp.int32)[None, :]
    shard_pick = (
        (z - jnp.arange(mp_size, dtype=jnp.int32)) % mp_size
    )[:, None] == jnp.arange(mp_size, dtype=jnp.int32)[None, :]

    def pick(flags, array, axis):
        moved = jnp.expand_dims(array, axis)
        shape = [1] * moved.ndim
        shape[axis], shape[axis + 1] = flags.shape
        return jnp.sum(jnp.where(flags.reshape(shape), moved, 0.0), axis=axis + 1)

    small = pick(shard_pick, small, 0)
    qv_bias = small[:, : 2 * local_width].reshape(mp_size, 2, heads, dp_size, strip)
    qv_bias = pick(slice_pick, qv_bias, 3).reshape(mp_size, 2, heads * HEAD)
    up_bias = pick(slice_pick, small[:, 2 * local_width :].reshape(mp_size, dp_size, span), 1)
    up_bias = up_bias.reshape(mp_size, hidden)

    b_out_f = b_out.astype(f32)
    gain_one_f = gain_one.astype(f32)
    shift_one_f = shift_one.astype(f32)
    b_down_f = b_down.astype(f32)
    gain_two_f = gain_two.astype(f32)
    w_head_f = w_head.astype(f32)
    b_head_f = b_head.astype(f32)

    own_tokens = lax.dynamic_slice_in_dim(tokens, row * seq, seq, 0)
    own_segments = slice_of(segment_ids, row, 0)
    own_length = slice_of(lengths, row, 0)
    own_cotangent = lax.dynamic_slice_in_dim(cotangent, row * seq, seq, 0) * active
    positions = jnp.arange(seq)
    valid = (positions < own_length).astype(f32)
    allowed = (own_segments[:, None] == own_segments[None, :]) & (
        (positions[:, None] < own_length) | (positions[:, None] == positions[None, :])
    )
    mask = jnp.where(allowed, 0.0, -1e30).astype(f32)

    part = heads * HEAD
    scale_col = jnp.concatenate([jnp.full((part,), HEAD**-0.5, f32), jnp.ones((2 * part,), f32)])
    qkv, context, probs = [], [], []
    branch = own_tokens.astype(f32) + b_out_f
    for k in range(mp_size):
        bias_col = jnp.concatenate([qv_bias[k, 0], jnp.zeros((part,), f32), qv_bias[k, 1]])
        w_k = attn_w[k][: 3 * heads].reshape(3 * part, width)
        made = (dot(w_k, own_tokens, 1, 1) + bias_col[:, None]) * scale_col[:, None]
        qkv.append(made.astype(bf16).reshape(3, heads, HEAD, seq))
        context_k, probs_k = attend(qkv[k], mask)
        context.append(context_k.reshape(part, seq))
        probs.append(probs_k)
        branch = branch + dot(context[k], attn_w[k][3 * heads :].reshape(part, width), 0, 0)
    scaled_one, normed_one, inv_one = layer_norm(branch, gain_one_f)
    norm_one = scaled_one + shift_one_f
    norm_one_low = norm_one.astype(bf16)
    pre, act = [], []
    res_two = norm_one + b_down_f
    for k in range(mp_size):
        pre.append(dot(norm_one_low, ffn_w[k][0], 1, 1) + up_bias[k])
        act.append(gelu_exact(pre[k]).astype(bf16))
        res_two = res_two + dot(act[k], ffn_w[k][1], 1, 0)
    norm_two, normed_two, inv_two = layer_norm(res_two, gain_two_f)
    logits = jnp.sum(norm_two * w_head_f, axis=-1) + b_head_f[0]
    own_weight = jax.nn.softplus(logits) * valid
    all_weights = lax.all_gather(own_weight, "mp")
    token_weight = jnp.concatenate([all_weights[i] for i in owners])

    d_logits = own_cotangent * valid * jax.nn.sigmoid(logits)
    grad_head = jnp.sum(d_logits[:, None] * norm_two, axis=0)
    grad_head_bias = jnp.sum(d_logits)[None]
    d_res_two, grad_gain_two, _ = norm_back(
        d_logits[:, None] * w_head_f, normed_two, inv_two, gain_two_f
    )
    grad_down_bias = jnp.sum(d_res_two, axis=0)
    d_res_two_low = d_res_two.astype(bf16)

    cut = hidden // 2
    d_norm_one = d_res_two
    grad_up_bias = [None] * mp_size
    ffn_going = None
    for k in later:
        d_hidden = dot(d_res_two_low, ffn_w[k][1], 1, 1) * gelu_slope(pre[k])
        grad_up_bias[k] = jnp.sum(d_hidden, axis=0)
        d_hidden_low = d_hidden.astype(bf16)
        sums = []
        for side, (left, right) in enumerate(((d_hidden_low, norm_one_low), (act[k], d_res_two_low))):
            got = links.swap(dot(left[:, cut:], right, 0, 0), CORE)
            kept = (dot(left[:, :cut], right, 0, 0) + got).reshape(half, span, width)
            parts = {m: kept[at] for at, m in enumerate(links.chip_masks)}
            sums.append(links.scatter(parts, side))
        if ffn_going is not None:
            sums = [one + two for one, two in zip(sums, ffn_going)]
        ffn_going = tuple(links.ring(one) for one in sums) if k else tuple(sums)
        d_norm_one = d_norm_one + dot(d_hidden_low, ffn_w[k][0], 1, 0)

    d_res_one, grad_gain_one, grad_shift_one = norm_back(
        d_norm_one, normed_one, inv_one, gain_one_f
    )
    grad_out_bias = jnp.sum(d_res_one, axis=0)
    d_res_one_low = d_res_one.astype(bf16)
    input_row = d_res_one
    grad_qv = [None] * mp_size
    attn_going = None
    for k in later:
        w_out_k = attn_w[k][3 * heads :].reshape(part, width)
        d_context = dot(w_out_k, d_res_one_low, 1, 1).astype(bf16).reshape(heads, HEAD, seq)
        d_qkv = attend_back(qkv[k], probs[k], context[k].reshape(heads, HEAD, seq), d_context)
        d_qkv_rows = d_qkv.reshape(3 * part, seq)
        grad_qv[k] = jnp.stack(
            [jnp.sum(d_qkv_rows[:part].astype(f32), axis=1), jnp.sum(d_qkv_rows[2 * part :].astype(f32), axis=1)]
        )
        input_row = input_row + dot(
            d_qkv_rows, attn_w[k][: 3 * heads].reshape(3 * part, width), 0, 0
        )
        grad_k = jnp.concatenate(
            [dot(d_qkv_rows, own_tokens, 1, 0), dot(context[k], d_res_one_low, 1, 0)]
        ).reshape(groups, 2, half, strip, width)
        sums = []
        for side in range(2):
            mine = grad_k[side * half_groups : (side + 1) * half_groups]
            got = links.swap(mine[:, 1], CORE)
            kept = mine[:, 0] + got
            parts = {m: kept[:, at] for at, m in enumerate(links.chip_masks)}
            sums.append(links.scatter(parts, side))
        if attn_going is not None:
            sums = [one + two for one, two in zip(sums, attn_going)]
        attn_going = tuple(links.ring(one) for one in sums) if k else tuple(sums)

    rows = {0: input_row}
    for k in range(1, mp_size):
        rows[k] = links.ring(rows[k - 1])
    input_grad = jnp.concatenate(
        [
            functools.reduce(
                lambda other, k: jnp.where((z - k) % mp_size == owner, rows[k], other),
                range(1, mp_size),
                rows[0],
            )
            for owner in owners
        ]
    )

    ffn_held = links.gather([one[None] for one in ffn_going])
    grad_up = natural(ffn_held[0], me).reshape(hidden, width).T
    grad_down = natural(ffn_held[1], me).reshape(hidden, width)
    attn_grad = jnp.concatenate([natural(held, me) for held in links.gather(attn_going)])
    grad_qkv = jnp.transpose(
        attn_grad[: 3 * heads].reshape(3, local_width, width), (2, 0, 1)
    )
    grad_out = attn_grad[3 * heads :].reshape(local_width, width)

    up_b = jnp.stack(grad_up_bias).reshape(mp_size, dp_size, span)
    up_b = pick(slice_pick.T, pick(shard_pick.T, up_b, 0), 1).reshape(-1)
    qv_b = jnp.stack(grad_qv).reshape(mp_size, 2, heads, dp_size, strip)
    qv_b = pick(slice_pick.T, pick(shard_pick.T, qv_b, 0), 3).reshape(-1)
    early = [up_b, grad_out_bias, grad_gain_one, grad_shift_one, grad_down_bias, grad_gain_two, grad_head, grad_head_bias]
    early_sum = lax.psum(jnp.concatenate(early), ("dp", "mp"))
    late_sum = lax.psum(qv_b, ("dp", "mp")).reshape(mp_size, 2, local_width)
    grad_qv_bias = slice_of(late_sum, z, 0)
    early_parts, at = [], 0
    for one in early:
        early_parts.append(early_sum[at : at + one.shape[0]])
        at += one.shape[0]
    grad_up_bias_out = slice_of(early_parts[0].reshape(mp_size, hidden), z, 0)
    (
        grad_out_bias,
        grad_gain_one,
        grad_shift_one,
        grad_down_bias,
        grad_gain_two,
        grad_head,
        grad_head_bias,
    ) = early_parts[1:]
    return (
        token_weight,
        input_grad,
        grad_qkv,
        grad_qv_bias,
        grad_out,
        grad_out_bias,
        grad_gain_one,
        grad_shift_one,
        grad_up,
        grad_up_bias_out,
        grad_down,
        grad_down_bias,
        grad_gain_two,
        grad_head,
        grad_head_bias,
    )


def solution(mesh):
    placed = (
        P("dp", None),
        P("dp", None),
        P("dp"),
        P("dp"),
        P(None, None, "mp"),
        P(None, "mp"),
        P("mp", None),
        P(),
        P(),
        P(),
        P(None, "mp"),
        P("mp"),
        P("mp", None),
        P(),
        P(),
        P(),
        P(),
    )
    return jax.shard_map(
        functools.partial(body, dp_size=mesh.shape["dp"], mp_size=mesh.shape["mp"]),
        mesh=mesh,
        in_specs=placed,
        out_specs=(
            P("dp"),
            P("dp", None),
            P(None, None, "mp"),
            P(None, "mp"),
            P("mp", None),
            P(),
            P(),
            P(),
            P(None, "mp"),
            P("mp"),
            P("mp", None),
            P(),
            P(),
            P(),
            P(),
        ),
        check_vma=False,
    )
```

```python
import functools

import jax
import jax.numpy as jnp
from jax import lax
from jax.experimental import pallas as pl
from jax.experimental.pallas import tpu as pltpu
from jax.sharding import PartitionSpec as P

HEAD = 64
CORE = 1
CHIP_BITS = (2, 4)
PLANE = 8
EVEN = (0, 2, 4, 6)
ALL = EVEN + tuple(m | CORE for m in EVEN)
norm_eps = 1e-12
highest = lax.Precision.HIGHEST
f32 = jnp.float32
bf16 = jnp.bfloat16


def dot(left, right, left_dim, right_dim):
    return lax.dot_general(
        left, right, (((left_dim,), (right_dim,)), ((), ())), preferred_element_type=f32
    )


def call(kernel, grid, ins, outs, scratch=(), name=None, micros=1, vmem=10):
    return pl.pallas_call(
        kernel,
        grid=grid,
        in_specs=[
            pl.BlockSpec(block, index, pipeline_mode=pl.Buffered(1))
            if index.__name__ == "once"
            else pl.BlockSpec(block, index)
            for _, block, index in ins
        ],
        out_specs=[pl.BlockSpec(block, index) for _, _, block, index in outs],
        out_shape=[jax.ShapeDtypeStruct(shape, dtype) for shape, dtype, _, _ in outs],
        scratch_shapes=list(scratch),
        compiler_params=pltpu.CompilerParams(vmem_limit_bytes=vmem << 20),
        cost_estimate=pl.CostEstimate(flops=0, bytes_accessed=int(micros * (1 << 21)), transcendentals=0),
        name=name,
    )(*[array for array, _, _ in ins])


def fixed(*zeros):
    def once(*_):
        return zeros

    return once


def by_mask(own_ref, got_ref, side):
    order = ((0, 1, 2, 3), (0, 2, 1, 3))[side]
    return jnp.concatenate([ref[at, 0] for ref in (own_ref, got_ref) for at in order])


def pack(arrays):
    first = arrays[0].shape
    total = sum(array.shape[0] for array in arrays)
    width = first[-1] // 2
    rest = first[1:-1]

    def kernel(*refs):
        at = 0
        for ref in refs[:-1]:
            refs[-1][at : at + ref.shape[0]] = ref[...]
            at += ref.shape[0]

    zeros = (0,) * (len(rest) + 1)
    index = lambda w: zeros + (w,)
    return call(
        kernel,
        (2,),
        [(array, (array.shape[0],) + rest + (width,), index) for array in arrays],
        [((total,) + first[1:], f32, (total,) + rest + (width,), index)],
        name="pack",
    )[0]


def attend(x, weights, bias, mask, shard):
    seq, width = x.shape
    heads, size = bias.shape[2:4]
    raw = isinstance(weights, tuple)

    def kernel(x_ref, bias_ref, mask_ref, *refs):
        count = 8 if raw else 1
        w_refs, outs = refs[:count], refs[count:]
        if raw:
            w = [
                by_mask(w_refs[at], w_refs[at + 4], at // 2).astype(bf16) for at in range(4)
            ]
            for at in range(4):
                outs[3][at, 0] = w[at]
            w = jnp.concatenate(w[:3])
        else:
            w = w_refs[0][:, 0].reshape(3 * size, width)
        qkv_ref, context_ref, probs_ref = outs[:3]
        made = dot(w, x_ref[...], 1, 1)
        query = ((made[:size] + bias_ref[0, 0, 0]) * HEAD**-0.5).astype(bf16)
        key = made[size : 2 * size].astype(bf16)
        value = (made[2 * size :] + bias_ref[0, 1, 0]).astype(bf16)
        qkv_ref[0, 0], qkv_ref[1, 0], qkv_ref[2, 0] = query, key, value
        scores = dot(key, query, 0, 0) + mask_ref[...]
        exponent = jnp.exp(scores - jnp.max(scores, axis=0, keepdims=True))
        probs = (exponent / jnp.sum(exponent, axis=0, keepdims=True)).astype(bf16)
        probs_ref[0] = probs
        context_ref[0] = dot(value, probs, 1, 0).astype(bf16)

    if raw:
        strip = weights[0].shape[2]
        w_ins = [
            (stack, (4, 1, strip, width), lambda h, at=at: (at // 2, at % 2 * heads + h, 0, 0))
            for stack in weights
            for at in range(4)
        ]
    else:
        w_ins = [(weights, (3, 1, size, width), lambda h: (0, h, 0, 0))]
    outs = [
        ((3, heads, size, seq), bf16, (3, 1, size, seq), lambda h: (0, h, 0, 0)),
        ((heads, size, seq), bf16, (1, size, seq), lambda h: (h, 0, 0)),
        ((heads, seq, seq), bf16, (1, seq, seq), lambda h: (h, 0, 0)),
    ]
    if raw:
        outs.append(((4, heads, size, width), bf16, (4, 1, size, width), lambda h: (0, h, 0, 0)))
    got = call(
        kernel,
        (heads,),
        [
            (x, (seq, width), fixed(0, 0)),
            (bias, (1, 2, 1, size, 1), lambda h: (shard, 0, h, 0, 0)),
            (mask, (seq, seq), fixed(0, 0)),
        ]
        + w_ins,
        outs,
        name="attend",
        micros=4,
        vmem=12,
    )
    return tuple(got) if raw else (*got, weights)


def attend_back(x, w, qkv, probs, context, low):
    heads, size, width = w.shape[1:]
    seq = x.shape[0]

    def kernel(x_ref, w_ref, qkv_ref, probs_ref, context_ref, low_ref, own_ref, peer_ref, d_qkv_ref, sums_ref):
        low_rows = low_ref[...]
        query, key, value = qkv_ref[0, 0], qkv_ref[1, 0], qkv_ref[2, 0]
        context_rows = context_ref[0]
        grad = dot(w_ref[0, 0], low_rows, 1, 1).astype(bf16)
        probs_rows = probs_ref[0]
        shared = jnp.sum(grad.astype(f32) * context_rows.astype(f32), axis=0, keepdims=True)
        d_scores = (probs_rows.astype(f32) * (dot(value, grad, 0, 0) - shared)).astype(bf16)
        d_query = (dot(key, d_scores, 1, 0) * HEAD**-0.5).astype(bf16)
        d_key = dot(query, d_scores, 1, 1).astype(bf16)
        d_value = dot(grad, probs_rows, 1, 1).astype(bf16)
        d_qkv_ref[0, 0], d_qkv_ref[1, 0], d_qkv_ref[2, 0] = d_query, d_key, d_value
        for at, one in enumerate((d_query, d_value)):
            sums_ref[at, 0] = jnp.sum(one.astype(f32), axis=1, keepdims=True)
        grads = dot(jnp.concatenate([d_query, d_key, d_value]), x_ref[...], 1, 0)
        grads = [grads[at * size : (at + 1) * size] for at in range(3)] + [dot(context_rows, low_rows, 1, 0)]
        for at, one in enumerate(grads):
            own_ref[at, 0], peer_ref[at, 0] = one[: size // 2], one[size // 2 :]

    half = ((4, heads, size // 2, width), f32, (4, 1, size // 2, width), lambda h: (0, h, 0, 0))
    return call(
        kernel,
        (heads,),
        [
            (x, (seq, width), fixed(0, 0)),
            (w, (1, 1, size, width), lambda h: (3, h, 0, 0)),
            (qkv, (3, 1, size, seq), lambda h: (0, h, 0, 0)),
            (probs, (1, seq, seq), lambda h: (h, 0, 0)),
            (context, (1, size, seq), lambda h: (h, 0, 0)),
            (low, (seq, width), fixed(0, 0)),
        ],
        [
            half,
            half,
            ((3, heads, size, seq), bf16, (3, 1, size, seq), lambda h: (0, h, 0, 0)),
            ((2, heads, size, 1), f32, (2, 1, size, 1), lambda h: (0, h, 0, 0)),
        ],
        name="attend_back",
        micros=0.05,
        vmem=12,
    )


def norm_one_rows(x, out_bias, contexts, weights, gain, shift):
    seq, width = x.shape
    step = seq // 2
    _, heads, size, _ = weights[0].shape
    part = heads * size
    count = len(weights)

    def kernel(x_ref, bias_ref, gain_ref, shift_ref, *refs):
        c_refs, w_refs = refs[:count], refs[count : 2 * count]
        out_ref, low_ref, normed_ref, inv_ref = refs[2 * count :]
        rows = x_ref[...].astype(f32) + bias_ref[...]
        for c_ref, w_ref in zip(c_refs, w_refs):
            rows = rows + dot(c_ref[...], w_ref[0].reshape(part, width), 0, 0)
        centered = rows - jnp.mean(rows, axis=1, keepdims=True)
        inv = lax.rsqrt(jnp.mean(centered * centered, axis=1, keepdims=True) + norm_eps)
        normed = centered * inv
        out = normed * gain_ref[...] + shift_ref[...]
        out_ref[...], low_ref[...], normed_ref[...], inv_ref[...] = out, out.astype(bf16), normed, inv

    rows = lambda i: (i, 0)
    row = (1, width)
    return call(
        kernel,
        (2,),
        [(x, (step, width), rows)]
        + [(vector, row, fixed(0, 0)) for vector in (out_bias, gain, shift)]
        + [(one.reshape(part, seq), (part, step), lambda i: (0, i)) for one in contexts]
        + [(w, (1, heads, size, width), fixed(3, 0, 0, 0)) for w in weights],
        [
            ((seq, width), f32, (step, width), rows),
            ((seq, width), bf16, (step, width), rows),
            ((seq, width), f32, (step, width), rows),
            ((seq, 1), f32, (step, 1), rows),
        ],
        name="norm_one",
        micros=2,
    )


def hidden_rows(low, weights, bias, total):
    seq, width = low.shape
    hidden = bias.shape[1]
    step = hidden // 2
    raw = weights[0].ndim == 4

    def kernel(low_ref, bias_ref, sum_ref, *refs):
        act_ref, slope_ref, out_ref = refs[4:7] if raw else refs[2:5]

        def run(up, down):
            pre = dot(low_ref[...], up, 1, 1) + bias_ref[...]
            half = 0.5 * (1.0 + lax.erf(pre * 0.7071067811865476))
            act = (pre * half).astype(bf16)
            act_ref[...] = act
            slope_ref[...] = half + pre * jnp.exp(-0.5 * pre * pre) * 0.3989422804014327
            return dot(act, down, 1, 0)

        for j in range(2):

            @pl.when(pl.program_id(0) == j)
            def _():
                if raw:
                    up_ref, down_ref = refs[2 * j : 2 * j + 2]
                    up = jnp.concatenate([up_ref[at, 0] for at in (0, 1, 2, 3)]).astype(bf16)
                    down = jnp.concatenate([down_ref[at, 0] for at in (0, 2, 1, 3)]).astype(bf16)
                    refs[7][...], refs[8][...] = up, down
                else:
                    up, down = refs[0][...], refs[1][...]
                part = run(up, down)
                if j:
                    out_ref[...] += part
                else:
                    out_ref[...] = sum_ref[...] + part

    if raw:
        strip = weights[0].shape[2]
        w_ins = [
            (stack, (4, 1, strip, width), fixed(side, 0, 0, 0)) for stack in weights for side in range(2)
        ]
    else:
        w_ins = [(w, (step, width), lambda j: (j, 0)) for w in weights]
    outs = [
        ((seq, hidden), bf16, (seq, step), lambda j: (0, j)),
        ((seq, hidden), f32, (seq, step), lambda j: (0, j)),
        ((seq, width), f32, (seq, width), fixed(0, 0)),
    ]
    if raw:
        outs += [((hidden, width), bf16, (step, width), lambda j: (j, 0))] * 2
    got = call(
        kernel,
        (2,),
        [
            (low, (seq, width), fixed(0, 0)),
            (bias, (1, step), lambda j: (0, j)),
            (total, (seq, width), fixed(0, 0)),
        ]
        + w_ins,
        outs,
        name="hidden_rows",
        micros=4,
        vmem=22 if raw else 14,
    )
    return tuple(got) if raw else (*got, *weights)


def hidden_back(half, low, norm_low, act, slope, down):
    seq, width = low.shape
    size = down.shape[0] // 2
    span = size // 4

    def kernel(low_ref, norm_ref, act_ref, slope_ref, down_ref, grad_ref, bias_ref, d_ref):
        @pl.when(pl.program_id(0) == 0)
        def _():
            d_hidden = dot(low_ref[...], down_ref[...], 1, 1) * slope_ref[...]
            bias_ref[...] = jnp.sum(d_hidden, axis=0, keepdims=True)
            d_low = d_hidden.astype(bf16)
            d_ref[...] = d_low
            grad_ref[...] = dot(d_low, norm_ref[...], 0, 0)

        @pl.when(pl.program_id(0) == 1)
        def _():
            grad = dot(act_ref[...], low_ref[...], 0, 0)
            grad_ref[...] = jnp.concatenate([grad[at * span : (at + 1) * span] for at in (0, 2, 1, 3)])

    return call(
        kernel,
        (2,),
        [
            (low, (seq, width), fixed(0, 0)),
            (norm_low, (seq, width), fixed(0, 0)),
            (act, (seq, size), fixed(0, half)),
            (slope, (seq, size), fixed(0, half)),
            (down, (size, width), fixed(half, 0)),
        ],
        [
            ((2 * size, width), f32, (size, width), lambda i: (i, 0)),
            ((1, size), f32, (1, size), fixed(0, 0)),
            ((seq, size), bf16, (seq, size), fixed(0, 0)),
        ],
        name="hidden_back",
        micros=0.05,
    )


def norm_one_back(grad, parts, ups, normed, inv, gain):
    seq, width = grad.shape
    step = seq // 2
    size = parts[0][0].shape[1]
    count = len(ups)

    def kernel(grad_ref, normed_ref, inv_ref, gain_ref, *refs):
        d_refs, up_refs = refs[: 2 * count], refs[2 * count : 3 * count]
        out_ref, low_ref, sums_ref = refs[3 * count :]
        rows, normed_rows = grad_ref[...], normed_ref[...]
        for at, d_ref in enumerate(d_refs):
            start = at % 2 * size
            rows = rows + dot(d_ref[...], up_refs[at // 2][start : start + size], 1, 0)
        g = rows * gain_ref[...]
        out = (
            g
            - jnp.mean(g, axis=1, keepdims=True)
            - normed_rows * jnp.mean(g * normed_rows, axis=1, keepdims=True)
        ) * inv_ref[...]
        out_ref[...] = out
        low_ref[...] = out.astype(bf16)
        sums = jnp.concatenate(
            [
                jnp.sum(out, axis=0, keepdims=True),
                jnp.sum(rows * normed_rows, axis=0, keepdims=True),
                jnp.sum(rows, axis=0, keepdims=True),
                jnp.zeros((5, width), f32),
            ]
        )

        @pl.when(pl.program_id(0) == 0)
        def _():
            sums_ref[...] = sums

        @pl.when(pl.program_id(0) > 0)
        def _():
            sums_ref[...] += sums

    at = lambda i: (i, 0)
    return call(
        kernel,
        (2,),
        [
            (grad, (step, width), at),
            (normed, (step, width), at),
            (inv, (step, 1), at),
            (gain, (1, width), fixed(0, 0)),
        ]
        + [(one, (step, size), at) for pair in parts for one in pair]
        + [(up, up.shape, fixed(0, 0)) for up in ups],
        [
            ((seq, width), f32, (step, width), at),
            ((seq, width), bf16, (step, width), at),
            ((8, width), f32, (8, width), fixed(0, 0)),
        ],
        name="norm_one_back",
        micros=0.05,
        vmem=14,
    )


def placed_rows(z, parts, owners, seq):
    count = len(parts[0])
    rows, width = parts[0][0].shape
    cuts = 3
    wide = width // cuts

    def kernel(z_ref, *refs):
        out_ref = refs[-1]
        for at, owner in enumerate(owners):
            back = lax.rem(z_ref[0] + count - owner, count)
            for p in range(len(parts)):
                start = at * seq + p * rows
                for k in range(count):

                    @pl.when(back == k)
                    def _():
                        out_ref[start : start + rows] = refs[p * count + k][...]

    arrays = [one for part in parts for one in part]
    return pl.pallas_call(
        kernel,
        grid=(cuts,),
        in_specs=[pl.BlockSpec(memory_space=pltpu.SMEM)]
        + [pl.BlockSpec((rows, wide), lambda c: (0, c))] * len(arrays),
        out_specs=pl.BlockSpec((len(owners) * seq, wide), lambda c: (0, c)),
        out_shape=jax.ShapeDtypeStruct((len(owners) * seq, width), f32),
        compiler_params=pltpu.CompilerParams(vmem_limit_bytes=32 << 20),
        cost_estimate=pl.CostEstimate(flops=0, bytes_accessed=1 << 20, transcendentals=0),
        name="placed_rows",
    )(z.astype(jnp.int32)[None], *arrays)


def input_rows(grad, parts, weights):
    seq, width = grad.shape
    step = seq // 2
    _, heads, size, _ = weights[0].shape
    part = 3 * heads * size
    count = len(weights)

    def kernel(grad_ref, *refs):
        rows = grad_ref[...]
        for d_ref, w_ref in zip(refs[:count], refs[count : 2 * count]):
            rows = rows + dot(d_ref[...], w_ref[...].reshape(part, width), 0, 0)
        refs[-1][...] = rows

    return call(
        kernel,
        (2,),
        [(grad, (step, width), lambda i: (i, 0))]
        + [(one.reshape(part, seq), (part, step), lambda i: (0, i)) for one in parts]
        + [(w, (3, heads, size, width), fixed(0, 0, 0, 0)) for w in weights],
        [((seq, width), f32, (step, width), lambda i: (i, 0))],
        name="input_rows",
        micros=0.05,
        vmem=12,
    )[0]


def head_rows(rows, gain, head, bias, cotangent, valid):
    seq, width = rows.shape
    step = seq // 2

    def kernel(bias_ref, rows_ref, gain_ref, head_ref, cot_ref, valid_ref, logits_ref, grad_ref, low_ref, sums_ref):
        res = rows_ref[...]
        centered = res - jnp.mean(res, axis=1, keepdims=True)
        inv = lax.rsqrt(jnp.mean(centered * centered, axis=1, keepdims=True) + norm_eps)
        normed = centered * inv
        gain_row, head_row = gain_ref[...], head_ref[...]
        norm_two = normed * gain_row
        logits = jnp.sum(norm_two * head_row, axis=1, keepdims=True) + bias_ref[0]
        logits_ref[...] = logits
        d_logits = cot_ref[...] * valid_ref[...] * lax.logistic(logits)
        d_norm = d_logits * head_row
        g = d_norm * gain_row
        grad = (g - jnp.mean(g, axis=1, keepdims=True) - normed * jnp.mean(g * normed, axis=1, keepdims=True)) * inv
        grad_ref[...] = grad
        low_ref[...] = grad.astype(bf16)
        sums = jnp.concatenate(
            [
                jnp.sum(grad, axis=0, keepdims=True),
                jnp.sum(d_norm * normed, axis=0, keepdims=True),
                jnp.sum(d_logits * norm_two, axis=0, keepdims=True),
                jnp.broadcast_to(jnp.sum(d_logits, axis=0, keepdims=True), (1, width)),
                jnp.zeros((4, width), f32),
            ]
        )

        @pl.when(pl.program_id(0) == 0)
        def _():
            sums_ref[...] = sums

        @pl.when(pl.program_id(0) > 0)
        def _():
            sums_ref[...] += sums

    at = lambda i: (i, 0)
    return pl.pallas_call(
        kernel,
        grid=(2,),
        in_specs=[
            pl.BlockSpec(memory_space=pltpu.SMEM),
            pl.BlockSpec((step, width), at),
            pl.BlockSpec((1, width), fixed(0, 0)),
            pl.BlockSpec((1, width), fixed(0, 0)),
            pl.BlockSpec((step, 1), at),
            pl.BlockSpec((step, 1), at),
        ],
        out_specs=[
            pl.BlockSpec((step, 1), at),
            pl.BlockSpec((step, width), at),
            pl.BlockSpec((step, width), at),
            pl.BlockSpec((8, width), fixed(0, 0)),
        ],
        out_shape=[
            jax.ShapeDtypeStruct((seq, 1), f32),
            jax.ShapeDtypeStruct((seq, width), f32),
            jax.ShapeDtypeStruct((seq, width), bf16),
            jax.ShapeDtypeStruct((8, width), f32),
        ],
        compiler_params=pltpu.CompilerParams(vmem_limit_bytes=16 << 20),
        cost_estimate=pl.CostEstimate(flops=0, bytes_accessed=1 << 16, transcendentals=0),
        name="head_rows",
    )(bias, rows, gain, head, cotangent, valid)


class Seg:
    def __init__(self, rows, terms):
        self.rows, self.terms = rows, tuple(terms)

    def __add__(self, other):
        return Seg(self.rows, self.terms + other.terms)


def rows_of(array, at, rows):
    return Seg(rows, [(array, (rows,), (at // rows,))])


def build_kernel(plan, counts, *refs):
    blocks, outs = refs[: counts[0]], refs[sum(counts) :]
    for out_ref, segments in zip(outs, plan):
        at = 0
        for rows, sources in segments:
            terms = [blocks[source][...] for source in sources]
            terms = [term.reshape(rows, term.shape[-1]) for term in terms]
            total = terms[0]
            for term in terms[1:]:
                total = total + term
            out_ref[at : at + rows] = total
            at += rows
    outs[-1][...] = jnp.zeros_like(outs[-1])


def hold(array):
    return lax.optimization_barrier(array)


class Links:
    def __init__(self, dp_size, mp_size):
        self.dp_size, self.mp_size = dp_size, mp_size
        self.orders = (CHIP_BITS, CHIP_BITS[::-1])

    def swap(self, array, bit):
        return hold(lax.ppermute(hold(array), "dp", [(i, i ^ bit) for i in range(self.dp_size)]))

    def ring(self, array):
        size = self.mp_size
        return hold(lax.ppermute(hold(array), "mp", [(i, (i + 1) % size) for i in range(size)]))

    def gather_plane(self, pieces, tie=()):
        stacks = [piece[None] for piece in pieces]
        for step in range(2):
            if step and tie:
                *stacks, tie = lax.optimization_barrier((*stacks, tie))
            got = [self.swap(stack, self.orders[side][step]) for side, stack in enumerate(stacks)]
            if step:
                return pack([stacks[0], got[0], stacks[1], got[1]]), tie
            stacks = [jnp.concatenate([one, two]) for one, two in zip(stacks, got)]


class Events:
    def __init__(self, dp_size, mp_size, width):
        self.dp_size, self.mp_size, self.width = dp_size, mp_size, width
        self.now = 0
        self.tasks = []
        self.results = {}
        self.token = jnp.zeros((8, 128), f32)
        self.needs = []
        self.later = []

    def add(self, name, steps, start):
        self.tasks.append([name, steps, start, None])

    def send(self, link, array):
        kind, amount = link
        size = self.dp_size if kind == "dp" else self.mp_size
        if kind == "dp":
            pairs = [(i, i ^ amount) for i in range(size)]
        elif kind in ("ring", "slow"):
            pairs = [(i, (i + amount) % size) for i in range(size)]
        elif kind == "swap":
            pairs = [(i, i ^ amount) for i in range(size)]
        else:
            pairs = list(amount)
        axis = "dp" if kind == "dp" else "mp"
        return hold(lax.ppermute(hold(array), axis, pairs))

    def build(self, messages):
        blocks, specs, plan = [], [], []
        cuts = 3
        wide = self.width // cuts
        known = {}
        for message in messages:
            segments = []
            for seg in message:
                sources = []
                for array, block, index in seg.terms:
                    key = (id(array), block, index)
                    if key not in known:
                        known[key] = len(blocks)
                        blocks.append(array)
                        specs.append(
                            pl.BlockSpec(block + (wide,), lambda c, index=index: index + (c,))
                        )
                    sources.append(known[key])
                segments.append((seg.rows, sources))
            plan.append(segments)
        others = [self.token] + self.needs
        self.needs = []
        sizes = [sum(seg.rows for seg in message) for message in messages]
        out = pl.pallas_call(
            functools.partial(build_kernel, plan, (len(blocks), len(others))),
            grid=(cuts,),
            in_specs=specs + [pl.BlockSpec(memory_space=pl.ANY)] * len(others),
            out_specs=[pl.BlockSpec((rows, wide), lambda c: (0, c)) for rows in sizes]
            + [pl.BlockSpec((8, 128), lambda c: (0, 0))],
            out_shape=[jax.ShapeDtypeStruct((rows, self.width), f32) for rows in sizes]
            + [jax.ShapeDtypeStruct((8, 128), f32)],
            compiler_params=pltpu.CompilerParams(vmem_limit_bytes=12 << 20),
            cost_estimate=pl.CostEstimate(flops=0, bytes_accessed=1 << 16, transcendentals=0),
            name="build",
        )(*blocks, *others)
        self.token = out[-1]
        return out[:-1]

    def step(self):
        asked = []
        at = 0
        while at < len(self.tasks):
            task = self.tasks[at]
            at += 1
            if task[2] != self.now:
                continue
            try:
                request = task[1].send(task[3])
            except StopIteration as end:
                self.results[task[0]] = end.value
                task[2] = -1
                continue
            task[2] = self.now + max([self.lag(link) for link, _ in request], default=1)
            task[3] = [[None] * len(segs) for _, segs in request]
            for part, (link, segs) in enumerate(request):
                for place, seg in enumerate(segs):
                    asked.append((link, seg, task[3][part], place))
        links = {}
        alone = []
        for one in asked:
            if isinstance(one[1], Seg):
                links.setdefault(one[0], []).append(one)
            else:
                alone.append(one)
        for ones in links.values():
            ones.sort(key=lambda one: -one[1].rows)
        self.needs = self.needs + [array for due, array in self.later if due <= self.now]
        self.later = [one for one in self.later if one[0] > self.now]
        built = []
        if links or self.needs:
            built = self.build([[one[1] for one in ones] for ones in links.values()])
        outgoing = [(link, ones, array) for (link, ones), array in zip(links.items(), built)]
        for link, array, into, place in alone:
            array, self.token = lax.optimization_barrier((array, self.token))
            outgoing.append((link, [(link, None, into, place)], array))
        outgoing.sort(key=lambda one: self.rank(one[0]))
        waiting = []
        for link, ones, array in outgoing:
            if False:
                array, waiting[-1] = lax.optimization_barrier((array, waiting[-1]))
            got = self.send(link, array)
            if self.lag(link) == 1:
                waiting.append(got)
            elif link[0] == "slow":
                self.later.append((self.now + 2, got))
            into_at = 0
            for _, seg, into, place in ones:
                if seg is None:
                    into[place] = got
                else:
                    into[place] = rows_of(got, into_at, seg.rows)
                    into_at += seg.rows
        self.needs = self.needs + waiting
        self.now += 1

    def lag(self, link):
        return 2 if link[0] == "slow" else 1

    def rank(self, link):
        if link[0] != "dp":
            return 3
        return 2 if link[1] == CORE else 1

    def until(self, *names):
        while any(name not in self.results for name in names):
            self.step()

    def after(self, *arrays):
        *arrays, self.token = lax.optimization_barrier((*arrays, self.token))
        return arrays if len(arrays) > 1 else arrays[0]


def gather_steps(first, second):
    held = ({0: first}, {0: second})
    for step in range(2):
        bits = (CHIP_BITS[step], CHIP_BITS[1 - step])
        got = yield [(("dp", bit), list(own.values())) for bit, own in zip(bits, held)]
        for bit, own, new in zip(bits, held, got):
            own.update({m ^ bit: seg for m, seg in zip(list(own), new)})
    got = yield [(("dp", CORE), list(held[0].values()) + list(held[1].values()))]
    for own, new in zip(held, (got[0][:4], got[0][4:])):
        own.update({m ^ CORE: seg for m, seg in zip(list(own), new)})
    return held


def scatter_steps(parts, extra_bits):
    for step in (1, 0):
        bits = (CHIP_BITS[step], CHIP_BITS[1 - step])
        kept = [[m for m in own if not m & bit] for bit, own in zip(bits, parts)]
        got = yield [
            (("dp", bit), [own[m | bit] for m in keep]) for bit, own, keep in zip(bits, parts, kept)
        ]
        parts = [
            {m: own[m] + seg for m, seg in zip(keep, new)}
            for own, keep, new in zip(parts, kept, got)
        ]
    sums = [own[0] for own in parts]
    for bit in extra_bits:
        got = yield [(("dp", bit), sums)]
        sums = [one + two for one, two in zip(sums, got[0])]
    return sums


def blocks_of(segs, wide):
    arrays, specs, plan = [], [], []
    for seg in segs:
        plan.append([])
        for array, block, index in seg.terms:
            plan[-1].append(len(arrays))
            arrays.append(array)
            specs.append(pl.BlockSpec(block + (wide,), lambda c, index=index: index + (c,)))
    return arrays, specs, plan


def natural_kernel(grouped, plan, me_ref, *refs):
    blocks, out_ref = refs[:-1], refs[-1]
    me = me_ref[0]
    for at, sources in enumerate(plan):
        mask = ALL[at % PLANE]
        wide = out_ref.shape[-1]
        terms = [blocks[source][...].reshape(-1, wide) for source in sources]
        total = terms[0]
        for term in terms[1:]:
            total = total + term
        rows = total.shape[0]
        if grouped:
            strip = grouped
            count = rows // strip
            start = pl.multiple_of((me ^ mask) * strip, 8)
            for g in range(count):
                out_ref[at // PLANE * count + g, pl.ds(start, strip)] = total[
                    g * strip : (g + 1) * strip
                ]
        else:
            out_ref[pl.ds(pl.multiple_of((me ^ mask) * rows, 8), rows)] = total


def natural(segs, me, grouped, out_dims):
    cuts = 2
    wide = out_dims[-1] // cuts
    arrays, specs, plan = blocks_of(segs, wide)
    lead = out_dims[:-1]
    return pl.pallas_call(
        functools.partial(natural_kernel, grouped, plan),
        grid=(cuts,),
        in_specs=[pl.BlockSpec(memory_space=pltpu.SMEM)] + specs,
        out_specs=pl.BlockSpec(lead + (wide,), lambda c: (0,) * len(lead) + (c,)),
        out_shape=jax.ShapeDtypeStruct(out_dims, f32),
        compiler_params=pltpu.CompilerParams(vmem_limit_bytes=14 << 20),
        cost_estimate=pl.CostEstimate(flops=0, bytes_accessed=1 << 20, transcendentals=0),
        name="natural",
    )(me.astype(jnp.int32)[None], *arrays)


def body(
    tokens,
    segment_ids,
    lengths,
    cotangent,
    w_qkv,
    b_qv,
    w_out,
    b_out,
    gain_one,
    shift_one,
    w_up,
    b_up,
    w_down,
    b_down,
    gain_two,
    w_head,
    b_head,
    *,
    dp_size,
    mp_size,
):
    row_count, seq = segment_ids.shape
    width = tokens.shape[1]
    local_width = w_qkv.shape[2]
    heads = local_width // HEAD
    hidden = w_up.shape[1]
    groups = 4 * heads
    half_groups = groups // 2
    strip = HEAD // PLANE
    span = hidden // PLANE
    half_rows = half_groups * strip
    links = Links(dp_size, mp_size)
    events = Events(dp_size, mp_size, width)
    extra_bits = [1 << b for b in range(3, dp_size.bit_length() - 1)]
    me = lax.axis_index("dp") % PLANE
    z = lax.axis_index("mp")
    later = list(range(1, mp_size)) + [0]

    owners = [i for i in range(mp_size) if i != mp_size // 2][:row_count]
    row_of = [owners.index(i) if i in owners else 0 for i in range(mp_size)]
    row = jnp.asarray(row_of, jnp.int32)[z]
    active = jnp.asarray([float(i in owners) for i in range(mp_size)], f32)[z]

    def slice_of(array, at, axis):
        return lax.dynamic_index_in_dim(array, at, axis, keepdims=False)

    attn_own = jnp.concatenate(
        [jnp.transpose(w_qkv, (1, 2, 0)).reshape(3 * heads, HEAD, width), w_out.reshape(heads, HEAD, width)]
    ).reshape(groups, PLANE, strip, width)
    up_own = w_up.T.reshape(PLANE, span, width)
    down_own = w_down.reshape(PLANE, span, width)
    small_width = 2 * local_width + hidden
    small_own = jnp.concatenate(
        [b_qv.astype(f32).reshape(-1), b_up.astype(f32), jnp.zeros((strip * width - small_width,), f32)]
    ).reshape(1, strip, width)
    attn_mine = jnp.concatenate([slice_of(attn_own, me, 1).astype(f32), small_own])
    ffn_mine = jnp.stack([slice_of(up_own, me, 0), slice_of(down_own, me, 0)]).astype(f32)

    def own_order(array, axis):
        return jnp.concatenate(
            [lax.dynamic_slice_in_dim(array, me ^ m, 1, axis) for m in ALL], axis=axis
        )

    attn_going, ffn_going = [attn_mine], [ffn_mine]
    attn_going.append(links.ring(attn_mine))
    ffn_going.append(links.ring(ffn_mine))
    (attn_going[1], attn_own, up_own, down_own, tokens, segment_ids, lengths, cotangent, b_out, gain_one, shift_one, b_down, gain_two, w_head, b_head) = (
        lax.optimization_barrier(
            (attn_going[1], attn_own, up_own, down_own, tokens, segment_ids, lengths, cotangent, b_out, gain_one, shift_one, b_down, gain_two, w_head, b_head)
        )
    )
    for k in range(2, mp_size):
        attn_going.append(links.ring(attn_going[-1]))
        ffn_going[-1], attn_going[-1] = lax.optimization_barrier((ffn_going[-1], attn_going[-1]))
        ffn_going.append(links.ring(ffn_going[-1]))
    attn_w = [own_order(attn_own, 1).reshape(4, heads, HEAD, width)]
    ffn_w = [[own_order(own, 0).reshape(hidden, width) for own in (up_own, down_own)]]
    smalls = [small_own]
    attn_held, ffn_held = [None], [None]
    for k in range(1, mp_size):
        smalls.append(attn_going[k][groups:])
        own, _ = links.gather_plane((attn_going[k][:half_groups], attn_going[k][half_groups:groups]))
        attn_held.append((own, links.swap(own, CORE)))
    slice_pick = (
        jnp.asarray(ALL, jnp.int32)[:, None] ^ me
    ) == jnp.arange(PLANE, dtype=jnp.int32)[None, :]
    shard_pick = (
        (z - jnp.arange(mp_size, dtype=jnp.int32)) % mp_size
    )[:, None] == jnp.arange(mp_size, dtype=jnp.int32)[None, :]

    def pick(flags, array, axis):
        moved = jnp.expand_dims(array, axis)
        shape = [1] * moved.ndim
        shape[axis], shape[axis + 1] = flags.shape
        return jnp.sum(jnp.where(flags.reshape(shape), moved, 0.0), axis=axis + 1)

    small = jnp.concatenate(smalls).reshape(mp_size, -1)
    qv_bias = small[:, : 2 * local_width].reshape(mp_size, 2, heads, PLANE, strip)
    qv_bias = pick(slice_pick, qv_bias, 3).reshape(mp_size, 2, heads, HEAD, 1)
    up_bias = pick(slice_pick, small[:, 2 * local_width : small_width].reshape(mp_size, PLANE, span), 1)
    up_bias = up_bias.reshape(mp_size, hidden)

    own_tokens = lax.dynamic_slice_in_dim(tokens, row * seq, seq, 0)
    own_segments = slice_of(segment_ids, row, 0)
    own_length = slice_of(lengths, row, 0)
    own_cotangent = lax.dynamic_slice_in_dim(cotangent, row * seq, seq, 0) * active
    positions = jnp.arange(seq)
    valid = (positions < own_length).astype(f32)
    allowed = (own_segments[:, None] == own_segments[None, :]) & (
        (positions[:, None] < own_length) | (positions[:, None] == positions[None, :])
    )
    mask = jnp.where(allowed, 0.0, -1e30).astype(f32)

    def wide_row(vector):
        return vector.astype(f32).reshape(1, -1)

    qkv, context, probs = [], [], []
    for k in range(mp_size):
        one, two, three, w_k = attend(own_tokens, attn_held[k] if k else attn_w[0], qv_bias, mask, k)
        if k:
            attn_w.append(w_k)
        qkv.append(one)
        context.append(two)
        probs.append(three)
    ties = {1: (), 2: (0, 1), 3: (2, 3)}
    for k in range(1, mp_size):
        tie = ties.get(k, ())
        stack, back = links.gather_plane(
            (ffn_going[k][0][None], ffn_going[k][1][None]), tuple(context[at] for at in tie)
        )
        for at, value in zip(tie, back):
            context[at] = value
        ffn_held.append(stack)
    norm_one, norm_one_low, normed_one, inv_one = norm_one_rows(
        own_tokens, wide_row(b_out), context, attn_w, wide_row(gain_one), wide_row(shift_one)
    )
    act, slope = [], []
    res_two = norm_one + b_down.astype(f32)
    for k in range(mp_size):
        if k == 1:
            ffn_held[1], res_two = lax.optimization_barrier((ffn_held[1], res_two))
        if k:
            ffn_held[k] = (ffn_held[k], links.swap(ffn_held[k], CORE))
        one, two, res_two, up_k, down_k = hidden_rows(
            norm_one_low, ffn_held[k] if k else ffn_w[0], up_bias[k].reshape(1, hidden), res_two
        )
        if k:
            ffn_w.append((up_k, down_k))
        act.append(one)
        slope.append(two)
    logits, d_res_two, d_res_two_low, head_sums = head_rows(
        res_two,
        wide_row(gain_two),
        wide_row(w_head),
        b_head.astype(f32),
        own_cotangent.reshape(seq, 1),
        valid.reshape(seq, 1),
    )
    own_weight = jax.nn.softplus(logits.reshape(seq)) * valid

    begin = events.now
    ffn_sums, attn_sums = {}, {}

    def ffn_scatter(k):
        own, peer = ffn_parts[k]
        ((got,),) = yield [(("dp", CORE), [peer])]
        parts = [
            {
                m: rows_of(own, (4 * side + at) * span, span) + rows_of(got, (4 * side + at) * span, span)
                for at, m in enumerate((EVEN, (0, 4, 2, 6))[side])
            }
            for side in range(2)
        ]
        sums = yield from scatter_steps(parts, [])
        ffn_sums[k] = sums

    def ring_sum(all_sums, link):
        while later[0] not in all_sums:
            yield []
        going = all_sums[later[0]]
        for k in later[1:]:
            (got,) = yield [(link, going)]
            while k not in all_sums:
                yield []
            going = [one + two for one, two in zip(all_sums[k], got)]
        for bit in extra_bits:
            (got,) = yield [(("dp", bit), going)]
            going = [one + two for one, two in zip(going, got)]
        return (yield from gather_steps(*going))

    def attn_scatter(k):
        own, peer = attn_parts[k]

        def piece(array, side, at):
            return Seg(half_rows, [(array, (half_groups, 1, strip), (side, at, 0))])

        ((got,),) = yield [(("dp", CORE), [peer])]
        got = got.reshape(own.shape)
        parts = [
            {m: piece(own, side, at) + piece(got, side, at) for at, m in enumerate(EVEN)}
            for side in range(2)
        ]
        sums = yield from scatter_steps(parts, [])
        attn_sums[k] = sums

    def small_sum():
        total = rows_of(small_own, 0, 16)
        for link in [("dp", CORE)] + [("dp", bit) for bit in CHIP_BITS] + [("dp", bit) for bit in extra_bits]:
            ((got,),) = yield [(link, [total])]
            total = total + got
        going, weights = total, [rows_of(weight_rows, 0, 8)]
        for _ in range(mp_size - 1):
            ((going, token),) = yield [(("ring", 1), [going, weights[-1]])]
            total = total + going
            weights.append(token)
        return total, weights

    grad_up_bias = [None] * mp_size
    ffn_parts, attn_parts, d_hidden = {}, {}, {}
    low = d_res_two_low
    events.add("ffn_final", ring_sum(ffn_sums, ("slow", 1)), 0)
    events.add("attn_final", ring_sum(attn_sums, ("ring", 1)), 0)

    def ffn_step(k):
        peer, bias_peer, d_peer = hidden_back(1, low, norm_one_low, act[k], slope[k], ffn_w[k][1])
        own, bias_own, d_own = hidden_back(0, low, norm_one_low, act[k], slope[k], ffn_w[k][1])
        grad_up_bias[k] = jnp.concatenate([bias_own, bias_peer], axis=1)
        d_hidden[k] = (d_own, d_peer)
        ffn_parts[k] = (own, peer)

    grad_qv = [None] * mp_size
    d_qkv = [None] * mp_size

    def attn_step(k):
        own, peer, d_qkv[k], grad_qv[k] = attend_back(own_tokens, attn_w[k], qkv[k], probs[k], context[k], low)
        attn_parts[k] = (own.reshape(groups, 4, strip, width), peer)

    def ffn_add(k):
        events.add("ffn_out%d" % k, ffn_scatter(k), events.now)

    def attn_add(k):
        events.add("attn_out%d" % k, attn_scatter(k), events.now)

    ffn_step(later[0])
    ffn_add(later[0])
    events.step()
    low = events.after(low)
    ffn_step(later[1])
    ffn_add(later[1])
    events.step()
    low = events.after(low)
    for k in later[2:]:
        ffn_step(k)
    ffn_add(later[2])
    events.step()
    d_res_two = events.after(d_res_two)
    d_res_one, low, norm_sums = norm_one_back(
        d_res_two,
        [d_hidden[k] for k in range(mp_size)],
        [ffn_w[k][0] for k in range(mp_size)],
        normed_one,
        inv_one,
        wide_row(gain_one),
    )
    ffn_add(later[3])
    events.step()
    low = events.after(low)
    attn_step(later[0])
    attn_step(later[1])
    attn_add(later[0])
    attn_add(later[1])
    events.step()
    low = events.after(low)
    attn_step(later[2])
    attn_step(later[3])
    input_row = input_rows(d_res_one, d_qkv, attn_w)
    attn_add(later[2])
    attn_add(later[3])

    half_seq = seq // 2
    rows = [[input_row[:half_seq]], [input_row[half_seq:]]]

    def hop(*parts):
        for part in parts:
            rows[part][-1] = events.after(rows[part][-1])
            rows[part].append(links.ring(rows[part][-1]))
            events.later.append((events.now + 1, rows[part][-1]))

    events.step()
    hop(0, 1)
    events.step()
    hop(0)
    events.step()
    up_b = jnp.stack(grad_up_bias).reshape(mp_size, PLANE, span)
    up_b = pick(slice_pick.T, pick(shard_pick.T, up_b, 0), 1).reshape(-1)
    qv_b = jnp.stack(grad_qv).reshape(mp_size, 2, heads, PLANE, strip)
    qv_b = pick(slice_pick.T, pick(shard_pick.T, qv_b, 0), 3).reshape(-1)
    parts = [up_b, qv_b]
    parts += [norm_sums[0], norm_sums[1], norm_sums[2], head_sums[0], head_sums[1], head_sums[2], head_sums[3, :1]]
    used = sum(one.shape[0] for one in parts)
    small_own = jnp.concatenate(parts + [jnp.zeros((16 * width - used,), f32)]).reshape(16, width)
    weight_rows = jnp.concatenate([own_weight, jnp.zeros((8 * width - seq,), f32)]).reshape(8, width)
    events.add("small", small_sum(), events.now)
    hop(1)
    events.step()
    events.step()
    events.step()
    events.step()
    hop(0)
    hop(1)
    events.until("ffn_final", "attn_final", "small")
    input_grad = placed_rows(z, rows, owners, seq)
    total, weights = events.results["small"]
    weights = [
        array[index[0] * 8 : (index[0] + 1) * 8] for one in weights for array, _, index in one.terms
    ]
    token_weight = []
    for owner in owners:
        value = weights[0]
        for k in range(1, mp_size):
            value = jnp.where((z - k) % mp_size == owner, weights[k], value)
        token_weight.append(value.reshape(-1)[:seq])
    token_weight = jnp.concatenate(token_weight)

    up_held, down_held = events.results["ffn_final"]
    grad_up = natural([up_held[m] for m in ALL], me, 0, (hidden, width)).T
    grad_down = natural([down_held[m] for m in ALL], me, 0, (hidden, width))
    one, two = events.results["attn_final"]
    attn_grad = natural([one[m] for m in ALL] + [two[m] for m in ALL], me, strip, (groups, HEAD, width))
    grad_qkv = jnp.transpose(
        attn_grad[: 3 * heads].reshape(3, local_width, width), (2, 0, 1)
    )
    grad_out = attn_grad[3 * heads :].reshape(local_width, width)

    small_total = sum(
        array[index[0] * block[0] : (index[0] + 1) * block[0]] for array, block, index in total.terms
    ).reshape(-1)
    sums, at = [], 0
    for one in parts:
        sums.append(small_total[at : at + one.shape[0]])
        at += one.shape[0]
    grad_up_bias_out = slice_of(sums[0].reshape(mp_size, hidden), z, 0)
    grad_qv_bias = slice_of(sums[1].reshape(mp_size, 2, local_width), z, 0)
    (
        grad_out_bias,
        grad_gain_one,
        grad_shift_one,
        grad_down_bias,
        grad_gain_two,
        grad_head,
        grad_head_bias,
    ) = sums[2:]
    return (
        token_weight,
        input_grad,
        grad_qkv,
        grad_qv_bias,
        grad_out,
        grad_out_bias,
        grad_gain_one,
        grad_shift_one,
        grad_up,
        grad_up_bias_out,
        grad_down,
        grad_down_bias,
        grad_gain_two,
        grad_head,
        grad_head_bias,
    )


def solution(mesh):
    placed = (
        P("dp", None),
        P("dp", None),
        P("dp"),
        P("dp"),
        P(None, None, "mp"),
        P(None, "mp"),
        P("mp", None),
        P(),
        P(),
        P(),
        P(None, "mp"),
        P("mp"),
        P("mp", None),
        P(),
        P(),
        P(),
        P(),
    )
    return jax.shard_map(
        functools.partial(body, dp_size=mesh.shape["dp"], mp_size=mesh.shape["mp"]),
        mesh=mesh,
        in_specs=placed,
        out_specs=(
            P("dp"),
            P("dp", None),
            P(None, None, "mp"),
            P(None, "mp"),
            P("mp", None),
            P(),
            P(),
            P(),
            P(None, "mp"),
            P("mp"),
            P("mp", None),
            P(),
            P(),
            P(),
            P(),
        ),
        check_vma=False,
    )
```
